32 devices in a mesh: seg: 8 (over y, x, core), stretch: 4 (over z).
Axes of the slice: x: 2, y: 2, z: 4, core: 2. Of those that a mesh axis runs over, the one named last changes fastest.
Arguments:
- queries: bfloat16 [1024, 8192], P('seg', 'stretch'), may hold values from -80 to 80
- branch_kv: bfloat16 [2, 1024, 1024], P(None, 'seg'), may hold values from -6 to 6
- prompt_kv: bfloat16 [2, 768, 1024], P(None, 'stretch'), may hold values from -4 to 4
- ancestry: int32 [8, 8], replicated, may hold values from 0 to 1, as said below
- segment_of_slot: int32 [8], replicated, may hold values from 0 to 7, each once
- counts: int32 [8], replicated, may hold values from 1 to 128, 768 in all
Outputs:
- attended: bfloat16 [1024, 8192], P('seg', 'stretch')
The draws below stay inside these ranges and needn't reach their ends.
Inputs may be any that keep to these rules, and one draw needn't show every extreme that they name: ancestry describes a tree rooted at segment 0 in which every segment's parent has a lower number: entry [a, b] is 1 exactly when b is a or an ancestor of a.
All inputs are finite; a program needn't handle non-finite values.
Results may differ from the reference program's by a relative error of at most 0.0085.
Values may be sent and summed in bfloat16 or wider, within the bound.
A program may use at most 64 MiB of HBM per device.

```python
import math
import jax
import jax.numpy as jnp
import numpy as np
from jax import lax

HEADS = 64
KV_HEADS = 8
HEAD_DIM = 128
BLOCK = 128
TOKENS = 1024
PROMPT = 768
N_SEG = 8


def shared_draw(key):
    base_key = jax.random.fold_in(key, 0)
    prompt_keys = jnp.clip(jax.random.normal(base_key, (PROMPT, KV_HEADS * HEAD_DIM), jnp.float32), -4.0, 4.0)
    return prompt_keys


def draw_prompt_kv(key, part):
    prompt_keys = shared_draw(key)
    key = jax.random.fold_in(key, 11)
    values = jnp.clip(jax.random.normal(key, prompt_keys.shape, jnp.float32), -4.0, 4.0)
    return jnp.stack([prompt_keys, values]).astype(jnp.bfloat16)


def draw_queries(key, part):
    key = jax.random.fold_in(key, 5)
    result = jnp.clip(jax.random.normal(key, (TOKENS, HEADS * HEAD_DIM), jnp.float32), -4.0, 4.0)
    return result.astype(jnp.bfloat16)


def draw_ancestry(key, part):
    key = jax.random.fold_in(key, 7)
    blocks = TOKENS // BLOCK
    labels = jnp.arange(blocks, dtype=jnp.int32)
    offsets = jax.random.randint(key, (blocks,), 1, 4)
    parent = jnp.maximum(labels - offsets, 0)
    identity = (labels[:, None] == labels[None, :]).astype(jnp.int32)
    nonroot = (labels[:, None] > 0).astype(jnp.int32)

    def extend(step_index, current):
        return jnp.maximum(identity, current[parent] * nonroot)
    return lax.fori_loop(0, blocks, extend, identity)


def block_levels(rng, dims, shards, least, top_value):
    def one(dim, parts):
        heights = jax.random.uniform(jax.random.fold_in(jax.random.fold_in(rng, 6), dim), (parts,), jnp.float32, least / len(shards), top_value / len(shards))
        return jnp.repeat(jnp.exp(heights), dims[dim] // parts).reshape((-1,) + (1,) * (len(dims) - dim - 1))

    factor_of = one(*shards[0])
    for cut in shards[1:]:
        factor_of = factor_of * one(*cut)
    return factor_of


def split_up(count, total, reach, skew):
    portions = [(1 << 20) // math.isqrt(rank ** skew) + 1 for rank in range(2, count + 1)]
    spare, given = total - reach - (count - 1), [1] * (count - 1)
    while spare > 0:
        movable = [i for i in range(count - 1) if given[i] < reach]
        pool, left = sum([portions[i] for i in movable]), spare
        for i in movable:
            extra = min(reach - given[i], max(1, left * portions[i] // pool), spare)
            given[i] = given[i] + extra
            spare = spare - extra
    return np.array([reach] + given)


def ragged_sizes(key, count, total, reach, slope):
    if count == 2:
        one = jax.random.randint(key, (), max(1, total - reach), min(reach, total - 1) + 1)
        return jnp.stack([one, total - one])
    sizes = jnp.asarray(split_up(count, total, reach, slope), jnp.int32)
    pairs = (count - 1) // 2
    source_of, receiver = sizes[1:1 + 2 * pairs:2], sizes[2:2 + 2 * pairs:2]
    room = jnp.minimum(source_of - 1, reach - receiver)
    moved = jax.random.randint(jax.random.fold_in(key, 1), (pairs,), 0, 1 << 20) % (room + 1)
    sizes = sizes.at[1:1 + 2 * pairs:2].set(source_of - moved).at[2:2 + 2 * pairs:2].set(receiver + moved)
    return sizes[jax.random.permutation(jax.random.fold_in(key, 2), count)]


def centred(rng, extent, width, bound, shards=(), kind=jnp.bfloat16):
    gain = block_levels(rng, extent, shards, -0.22, 0.18) if shards else 1.0
    values = jax.random.normal(rng, extent, jnp.float32) * width * gain
    return jnp.minimum(jnp.maximum(values, -bound), bound).astype(kind)


def setup_inputs(seed: int = 0) -> dict:
    key_list = jax.random.split(jax.random.key(seed), 7)
    return {
        "queries": draw_queries(jax.random.fold_in(key_list[6], 71), 0),
        "branch_kv": centred(key_list[1], (2, TOKENS, KV_HEADS * HEAD_DIM), 1.0, 6.0, ((1, 8),)),
        "prompt_kv": draw_prompt_kv(jax.random.fold_in(key_list[6], 71), 0),
        "ancestry": draw_ancestry(jax.random.fold_in(key_list[6], 71), 0),
        "segment_of_slot": jax.random.permutation(key_list[4], N_SEG).astype(jnp.int32),
        "counts": ragged_sizes(key_list[5], N_SEG, N_SEG * BLOCK * 3 // 4, BLOCK, 0).astype(jnp.int32),
    }


def reference(queries, branch_kv, prompt_kv, ancestry, segment_of_slot, counts):
    group_size = HEADS // KV_HEADS
    blocks = TOKENS // BLOCK
    score_scale = 1.0 / math.sqrt(HEAD_DIM)
    slot_links = ancestry[segment_of_slot][:, segment_of_slot]
    slot_counts = counts[segment_of_slot]
    positions = jnp.arange(BLOCK, dtype=jnp.int32)
    key_live = positions[None, :] < slot_counts[:, None]
    prompt_keys = prompt_kv[0].astype(jnp.float32).reshape(PROMPT, KV_HEADS, HEAD_DIM)
    prompt_values = prompt_kv[1].astype(jnp.float32).reshape(PROMPT, KV_HEADS, HEAD_DIM)
    branch_keys = branch_kv[0].astype(jnp.float32).reshape(blocks, BLOCK, KV_HEADS, HEAD_DIM)
    branch_values = branch_kv[1].astype(jnp.float32).reshape(blocks, BLOCK, KV_HEADS, HEAD_DIM)
    slot_ids = jnp.arange(blocks, dtype=jnp.int32)

    def one_block(slot_index):
        query_rows = lax.dynamic_slice_in_dim(queries, slot_index * BLOCK, BLOCK, 0)
        query_rows = query_rows.astype(jnp.float32).reshape(BLOCK, KV_HEADS, group_size, HEAD_DIM)
        prompt_scores = jnp.einsum('pgrd,tgd->pgrt', query_rows, prompt_keys) * score_scale
        branch_scores = jnp.einsum('pgrd,sugd->pgrsu', query_rows, branch_keys) * score_scale
        linked = lax.dynamic_index_in_dim(slot_links, slot_index, 0, keepdims=False) > 0
        other_slot = slot_ids[None, :, None] != slot_index
        causal = positions[None, None, :] <= positions[:, None, None]
        allowed = linked[None, :, None] & key_live[None] & (other_slot | causal)
        visible = allowed[:, None, None]
        branch_scores = jnp.where(visible, branch_scores, -jnp.inf)
        peak = jnp.maximum(lax.optimization_barrier(jnp.max(prompt_scores, -1)), lax.optimization_barrier(jnp.max(branch_scores, axis=(-2, -1))))
        prompt_weights = jnp.exp(prompt_scores - peak[..., None])
        branch_weights = jnp.where(visible, jnp.exp(branch_scores - peak[..., None, None]), 0.0)
        totals = lax.optimization_barrier(jnp.sum(prompt_weights, -1)) + lax.optimization_barrier(jnp.sum(branch_weights, axis=(-2, -1)))
        prompt_short = lax.optimization_barrier(prompt_weights.astype(jnp.bfloat16)).astype(jnp.float32)
        branch_short = lax.optimization_barrier(branch_weights.astype(jnp.bfloat16)).astype(jnp.float32)
        blended = jnp.einsum('pgrt,tgd->pgrd', prompt_short, prompt_values)
        blended = blended + jnp.einsum('pgrsu,sugd->pgrd', branch_short, branch_values)
        result = (blended / totals[..., None]).astype(jnp.bfloat16)
        return result.reshape(BLOCK, HEADS * HEAD_DIM)
    return lax.map(one_block, slot_ids).reshape(TOKENS, HEADS * HEAD_DIM)
```

```python
import functools
import math

import jax
import jax.numpy as jnp
from jax import lax
from jax.experimental import pallas as pl
from jax.experimental.pallas import tpu as pltpu
from jax.sharding import PartitionSpec as P

HEADS = 64
KV_HEADS = 8
HEAD_DIM = 128
GROUP = HEADS // KV_HEADS
CUBE = 8
EXP2_SCALE = math.log2(math.e) / math.sqrt(HEAD_DIM)
HIDDEN = -1e30

OWN, SIB, A, B, SIB_A, SIB_B, DIAG, SIB_DIAG = range(8)


def kernel(
    seg_count, stretch_count, block_rows,
    anc_ref, seg_ref, cnt_ref, q_hbm, branch_hbm, prompt_hbm, out_ref,
    q_ref, own_prompt, branch, prompt, peak_ref, acc_ref, tot_ref,
    local_sem, z_send, z_recv, g_send, g_recv, b_send, b_recv, p_send, p_recv,
):
    per_dev = q_hbm.shape[1] // HEAD_DIM
    rows = q_hbm.shape[0]
    kv_per = max(1, per_dev // GROUP)
    sub = per_dev // kv_per
    width = kv_per * HEAD_DIM
    groups = seg_count // CUBE
    part = prompt_hbm.shape[1] // (CUBE // 2)

    s = lax.axis_index("seg")
    z = lax.axis_index("stretch")
    g, r = s // CUBE, s % CUBE
    chip, c = r // 2, r % 2
    y, x = r // 4, (r // 2) % 2
    dx, dy, dc = 2 - 4 * x, 4 - 8 * y, 1 - 2 * c
    da = (1 - c) * dx + c * dy
    db = c * dx + (1 - c) * dy
    to_a, to_b, to_sib = {"seg": s + da}, {"seg": s + db}, {"seg": s + dc}
    at_a, at_b = 1 + c, 2 - c

    def columns(stretch):
        first = stretch * per_dev // GROUP
        return pl.ds(pl.multiple_of(first * HEAD_DIM, HEAD_DIM), width)

    loads = [
        pltpu.make_async_copy(q_hbm, q_ref, local_sem.at[0]),
        pltpu.make_async_copy(branch_hbm.at[:, :, columns(z)], branch.at[OWN, 0], local_sem.at[1]),
        pltpu.make_async_copy(prompt_hbm.at[:, :, columns(z)], own_prompt, local_sem.at[2]),
    ]
    barrier = pltpu.get_barrier_semaphore()
    partners = [to_a, to_b, to_sib]
    partners += [{"stretch": (z + j) % stretch_count} for j in range(1, stretch_count)]
    partners += [{"seg": (g + j) % groups * CUBE + r} for j in range(1, groups)]
    for partner in partners:
        pl.semaphore_signal(barrier, inc=1, device_id=partner, device_id_type=pl.DeviceIdType.MESH)
    for load in loads:
        load.start()
    pl.semaphore_wait(barrier, len(partners))

    sent = []

    def send(source, target, send_sem, recv_sem, device):
        copy = pltpu.make_async_remote_copy(
            src_ref=source, dst_ref=target, send_sem=send_sem, recv_sem=recv_sem,
            device_id=device, device_id_type=pl.DeviceIdType.MESH,
        )
        copy.start()
        sent.append(copy)

    def arrived(target, recv_sem):
        pltpu.make_async_copy(target, target, recv_sem).wait()

    quarter = pl.ds(pl.multiple_of(chip * part, 16), part)
    for j in range(1, stretch_count):
        other = (z + stretch_count - j) % stretch_count
        send(
            prompt_hbm.at[c, quarter, columns(other)], prompt.at[c, 0, j - 1],
            z_send.at[j - 1], z_recv.at[j - 1], {"stretch": other},
        )
    for j in range(1, groups):
        send(
            branch_hbm.at[:, :, columns(z)], branch.at[OWN, j],
            g_send.at[j - 1], g_recv.at[j - 1], {"seg": (g + groups - j) % groups * CUBE + r},
        )
    if groups > 1:
        loads[1].wait()
        for j in range(1, groups):
            arrived(branch.at[OWN, j], g_recv.at[j - 1])

    def branch_part(slot, kind):
        return branch.at[slot, :, kind]

    def send_branch(slot, kind, target, device):
        if groups == 1 and slot == OWN:
            source = branch_hbm.at[kind, :, columns(z)]
            place = branch.at[target, 0, kind]
        else:
            source, place = branch_part(slot, kind), branch_part(target, kind)
        send(source, place, b_send.at[target, kind], b_recv.at[target, kind], device)

    def branch_arrived(slot, kind):
        arrived(branch_part(slot, kind), b_recv.at[slot, kind])

    for kind in range(2):
        send_branch(OWN, kind, A, to_a)
        send_branch(OWN, kind, SIB, to_sib)
    for kind in range(2):
        send_branch(OWN, kind, B, to_b)

    def send_prompt(place, target_place, message, device):
        send(prompt.at[c, place], prompt.at[c, target_place], p_send.at[message], p_recv.at[message], device)

    def prompt_arrived(kind, place, message):
        arrived(prompt.at[kind, place], p_recv.at[message])

    def linked_rows(rank, j):
        slot = (g + j) % groups * CUBE + rank
        segment = seg_ref[slot]
        return anc_ref[seg_ref[s], segment] * cnt_ref[segment]

    ranks = {
        OWN: r, SIB: r + dc, A: r + da, B: r + db, SIB_A: r + dc + db, SIB_B: r + dc + da,
        DIAG: r + da + db, SIB_DIAG: r + dc + da + db,
    }
    ones = jnp.ones((1, HEAD_DIM), jnp.float32)

    def operands(slots, h):
        cols = slice(h * HEAD_DIM, (h + 1) * HEAD_DIM)
        first_key = own_prompt[0, 0:16, cols].astype(jnp.float32)[0:1]
        keys, values = [], []
        place = lax.broadcasted_iota(jnp.int32, (rows, HEAD_DIM), 0)
        for slot in slots:
            for j in range(groups):
                live = place < linked_rows(ranks[slot], j)
                key = branch[slot, j, 0, :, cols].astype(jnp.float32)
                value = branch[slot, j, 1, :, cols].astype(jnp.float32)
                keys.append(jnp.where(live, key, first_key).astype(jnp.bfloat16))
                values.append(
                    jnp.concatenate([jnp.where(live, value, 0.0), jnp.where(live, 1.0, 0.0)], 1).astype(jnp.bfloat16)
                )
        return jnp.concatenate(keys, 0), jnp.concatenate(values, 0)

    def prompt_operands(h):
        cols = slice(h * HEAD_DIM, (h + 1) * HEAD_DIM)
        count = (CUBE // 2) * (stretch_count - 1) * part
        out = []
        for kind in range(2):
            out.append(jnp.concatenate([own_prompt[kind, :, cols], prompt[kind, :, :, :, cols].reshape(count, HEAD_DIM)], 0))
        keys, values = out
        return keys, jnp.concatenate([values, jnp.ones_like(values)], 1)

    def attend(h, keys, values, first=False, last=False):
        count = keys.shape[0]
        heads = block_rows // rows
        for start in range(0, sub, heads):
            span = slice(start * rows, (start + heads) * rows)
            query = jnp.concatenate(
                [q_ref[:, (h * sub + i) * HEAD_DIM:(h * sub + i + 1) * HEAD_DIM] for i in range(start, start + heads)], 0
            )
            scores = lax.dot_general(query, keys, (((1,), (1,)), ((), ())), preferred_element_type=jnp.float32)
            tiles = [scores[:, t:t + HEAD_DIM] for t in range(0, count, HEAD_DIM)]
            if first:
                causal = lax.broadcasted_iota(jnp.int32, (block_rows, HEAD_DIM), 1) <= (
                    lax.broadcasted_iota(jnp.int32, (block_rows, HEAD_DIM), 0) % rows
                )
                tiles[0] = jnp.where(causal, tiles[0], HIDDEN)
            top = functools.reduce(jnp.maximum, tiles)
            peak = jnp.max(top, -1, keepdims=True)
            if first:
                peak = jnp.broadcast_to(peak, (block_rows, HEAD_DIM))
            else:
                former = peak_ref[h, span]
                peak = jnp.maximum(former, peak)
            weights = jnp.concatenate([jnp.exp2((tile - peak) * EXP2_SCALE).astype(jnp.bfloat16) for tile in tiles], 1)
            both = lax.dot_general(weights, values, (((1,), (0,)), ((), ())), preferred_element_type=jnp.float32)
            acc, tot = both[:, :HEAD_DIM], both[:, HEAD_DIM:]
            if not first:
                scale = jnp.exp2((former - peak) * EXP2_SCALE)
                acc = acc + acc_ref[h, span] * scale
                tot = tot + tot_ref[h, span] * scale
            if last:
                result = (acc / tot).astype(jnp.bfloat16)
                for i in range(heads):
                    head = h * sub + start + i
                    out_ref[:, head * HEAD_DIM:(head + 1) * HEAD_DIM] = result[i * rows:(i + 1) * rows]
            else:
                peak_ref[h, span] = peak
                acc_ref[h, span] = acc
                tot_ref[h, span] = tot

    loads[0].wait()
    if groups == 1:
        loads[1].wait()
    loads[2].wait()
    for kind in range(2):
        branch_arrived(SIB, kind)
    for h in range(kv_per):
        attend(h, *operands([OWN, SIB] if groups == 1 else [OWN], h), first=True)
    for j in range(1, stretch_count):
        arrived(prompt.at[c, 0, j - 1], z_recv.at[j - 1])
    send_prompt(0, at_a, 0, to_a)
    send_prompt(0, at_b, 1, to_b)
    send_prompt(0, 0, 3, to_sib)
    for kind in range(2):
        branch_arrived(A, kind)
        send_branch(A, kind, DIAG, to_b)
        send_branch(A, kind, SIB_A, to_sib)
    for kind in range(2):
        branch_arrived(B, kind)
        send_branch(B, kind, SIB_B, to_sib)
    for slot in (SIB_A, SIB_B):
        for kind in range(2):
            branch_arrived(slot, kind)
    near = [A, B, SIB_A, SIB_B]
    if groups > 1:
        near = [SIB] + near
    attend(0, *operands(near, 0))
    prompt_arrived(c, at_a, 0)
    send_prompt(at_a, 3, 2, to_b)
    send_prompt(at_a, at_a, 4, to_sib)
    prompt_arrived(c, at_b, 1)
    send_prompt(at_b, at_b, 5, to_sib)
    for kind in range(2):
        branch_arrived(DIAG, kind)
        send_branch(DIAG, kind, SIB_DIAG, to_sib)
    for h in range(1, kv_per):
        attend(h, *operands(near, h))
    prompt_arrived(c, 3, 2)
    send_prompt(3, 3, 6, to_sib)
    for kind in range(2):
        branch_arrived(SIB_DIAG, kind)
    for h in range(kv_per):
        attend(h, *operands([DIAG, SIB_DIAG], h))
    prompt_arrived(1 - c, 0, 3)
    prompt_arrived(1 - c, at_b, 4)
    prompt_arrived(1 - c, at_a, 5)
    prompt_arrived(1 - c, 3, 6)
    for h in range(kv_per):
        attend(h, *prompt_operands(h), last=True)
    for copy in sent:
        copy.wait_send()


def local(queries, branch_kv, prompt_kv, ancestry, segment_of_slot, counts):
    seg_count = lax.axis_size("seg")
    stretch_count = lax.axis_size("stretch")
    rows, features = queries.shape
    per_dev = features // HEAD_DIM
    kv_per = max(1, per_dev // GROUP)
    sub = per_dev // kv_per
    width = kv_per * HEAD_DIM
    groups = seg_count // CUBE
    part = prompt_kv.shape[1] // (CUBE // 2)
    state = pltpu.VMEM((kv_per, sub * rows, HEAD_DIM), jnp.float32)
    dma = pltpu.SemaphoreType.DMA
    smem = pl.BlockSpec(memory_space=pltpu.SMEM)
    hbm = pl.BlockSpec(memory_space=pl.ANY)
    return pl.pallas_call(
        functools.partial(kernel, seg_count, stretch_count, min(sub, 4) * rows),
        out_shape=jax.ShapeDtypeStruct((rows, features), jnp.bfloat16),
        in_specs=[smem, smem, smem, hbm, hbm, hbm],
        out_specs=pl.BlockSpec(memory_space=pltpu.VMEM),
        scratch_shapes=[
            pltpu.VMEM((rows, features), jnp.bfloat16),
            pltpu.VMEM((2, prompt_kv.shape[1], width), jnp.bfloat16),
            pltpu.VMEM((CUBE, groups, 2, rows, width), jnp.bfloat16),
            pltpu.VMEM((2, CUBE // 2, stretch_count - 1, part, width), jnp.bfloat16),
            state, state, state,
            dma((3,)),
            dma((stretch_count - 1,)), dma((stretch_count - 1,)),
            dma((max(1, groups - 1),)), dma((max(1, groups - 1),)),
            dma((8, 2)), dma((8, 2)),
            dma((7,)), dma((7,)),
        ],
        compiler_params=pltpu.CompilerParams(
            collective_id=0, has_side_effects=True, vmem_limit_bytes=40 * 1024 * 1024
        ),
    )(ancestry, segment_of_slot, counts, queries, branch_kv, prompt_kv)


def solution(mesh):
    return jax.shard_map(
        local,
        mesh=mesh,
        in_specs=(
            P("seg", "stretch"),
            P(None, "seg", None),
            P(None, "stretch", None),
            P(),
            P(),
            P(),
        ),
        out_specs=P("seg", "stretch"),
        check_vma=False,
    )
```

```python
import functools
import math

import jax
import jax.numpy as jnp
from jax import lax
from jax.experimental import pallas as pl
from jax.experimental.pallas import tpu as pltpu
from jax.sharding import PartitionSpec as P

HEADS = 64
KV_HEADS = 8
HEAD_DIM = 128
GROUP = HEADS // KV_HEADS
CUBE = 8
EXP2_SCALE = math.log2(math.e) / math.sqrt(HEAD_DIM)
HIDDEN = -1e30

OWN, SIB, A, B, SIB_A, SIB_B, DIAG, SIB_DIAG = range(8)


def kernel(
    seg_count, stretch_count, block_rows,
    anc_hbm, seg_hbm, cnt_hbm, q_hbm, branch_hbm, prompt_hbm, out_ref,
    anc_ref, seg_ref, cnt_ref,
    q_ref, own_prompt, branch, prompt, peak_ref, acc_ref, tot_ref,
    local_sem, z_send, z_recv, g_send, g_recv, b_send, b_recv, p_send, p_recv,
):
    per_dev = q_hbm.shape[1] // HEAD_DIM
    rows = q_hbm.shape[0]
    kv_per = max(1, per_dev // GROUP)
    sub = per_dev // kv_per
    width = kv_per * HEAD_DIM
    groups = seg_count // CUBE

    s = lax.axis_index("seg")
    z = lax.axis_index("stretch")
    g, r = s // CUBE, s % CUBE
    c = r % 2
    y, x = r // 4, (r // 2) % 2
    dx, dy, dc = 2 - 4 * x, 4 - 8 * y, 1 - 2 * c
    da = (1 - c) * dx + c * dy
    db = c * dx + (1 - c) * dy
    to_a, to_b, to_sib = {"seg": s + da}, {"seg": s + db}, {"seg": s + dc}
    to_diag = {"seg": s + da + db}

    def columns(stretch):
        first = stretch * per_dev // GROUP
        return pl.ds(pl.multiple_of(first * HEAD_DIM, HEAD_DIM), width)

    loads = [
        pltpu.make_async_copy(q_hbm, q_ref, local_sem.at[0]),
        pltpu.make_async_copy(branch_hbm.at[:, :, columns(z)], branch.at[OWN, 0], local_sem.at[1]),
        pltpu.make_async_copy(prompt_hbm.at[:, :, columns(z)], own_prompt, local_sem.at[2]),
        pltpu.make_async_copy(anc_hbm, anc_ref, local_sem.at[3]),
        pltpu.make_async_copy(seg_hbm, seg_ref, local_sem.at[4]),
        pltpu.make_async_copy(cnt_hbm, cnt_ref, local_sem.at[5]),
    ]
    barrier = pltpu.get_barrier_semaphore()
    partners = [to_a, to_b, to_sib, to_diag]
    partners += [{"stretch": (z + j) % stretch_count} for j in range(1, stretch_count)]
    partners += [{"seg": (g + j) % groups * CUBE + r} for j in range(1, groups)]
    for partner in partners:
        pl.semaphore_signal(barrier, inc=1, device_id=partner, device_id_type=pl.DeviceIdType.MESH)
    for load in loads:
        load.start()
    pl.semaphore_wait(barrier, len(partners))

    sent = []

    def send(source, target, send_sem, recv_sem, device):
        copy = pltpu.make_async_remote_copy(
            src_ref=source, dst_ref=target, send_sem=send_sem, recv_sem=recv_sem,
            device_id=device, device_id_type=pl.DeviceIdType.MESH,
        )
        copy.start()
        sent.append(copy)

    def arrived(target, recv_sem):
        pltpu.make_async_copy(target, target, recv_sem).wait()

    order = list(range(1, stretch_count))
    order.sort(key=lambda j: abs(2 * j - stretch_count))
    for j in order:
        other = (z + stretch_count - j) % stretch_count
        send(
            prompt_hbm.at[c, :, columns(other)], prompt.at[c, j - 1],
            z_send.at[j - 1], z_recv.at[j - 1], {"stretch": other},
        )
    for j in range(1, groups):
        send(
            branch_hbm.at[:, :, columns(z)], branch.at[OWN, j],
            g_send.at[j - 1], g_recv.at[j - 1], {"seg": (g + groups - j) % groups * CUBE + r},
        )
    if groups > 1:
        loads[1].wait()
        for j in range(1, groups):
            arrived(branch.at[OWN, j], g_recv.at[j - 1])

    def branch_part(slot, kind):
        return branch.at[slot, :, kind]

    def send_branch(slot, kind, target, device):
        if groups == 1 and slot == OWN:
            source = branch_hbm.at[kind, :, columns(z)]
            place = branch.at[target, 0, kind]
        else:
            source, place = branch_part(slot, kind), branch_part(target, kind)
        send(source, place, b_send.at[target, kind], b_recv.at[target, kind], device)

    def branch_arrived(slot, kind):
        arrived(branch_part(slot, kind), b_recv.at[slot, kind])

    for kind in range(2):
        send_branch(OWN, kind, A, to_a)
        send_branch(OWN, kind, SIB, to_sib)
    for kind in range(2):
        send_branch(OWN, kind, B, to_b)
    for kind in range(2):
        send_branch(OWN, kind, DIAG, to_diag)

    def pass_prompt(j):
        arrived(prompt.at[c, j - 1], z_recv.at[j - 1])
        send(prompt.at[c, j - 1], prompt.at[c, j - 1], p_send.at[j - 1], p_recv.at[j - 1], to_sib)

    def pass_branch(slot, target):
        for kind in range(2):
            branch_arrived(slot, kind)
            send_branch(slot, kind, target, to_sib)

    def prompt_passed(j):
        arrived(prompt.at[1 - c, j - 1], p_recv.at[j - 1])

    def linked_rows(rank, j):
        slot = (g + j) % groups * CUBE + rank
        segment = seg_ref[slot]
        return anc_ref[seg_ref[s], segment] * cnt_ref[segment]

    ranks = {
        OWN: r, SIB: r + dc, A: r + da, B: r + db, SIB_A: r + dc + db, SIB_B: r + dc + da,
        DIAG: r + da + db, SIB_DIAG: r + dc + da + db,
    }
    ones = jnp.ones((1, HEAD_DIM), jnp.float32)

    def operands(slots, h):
        cols = slice(h * HEAD_DIM, (h + 1) * HEAD_DIM)
        first_key = own_prompt[0, 0:16, cols].astype(jnp.float32)[0:1]
        keys, values = [], []
        place = lax.broadcasted_iota(jnp.int32, (rows, HEAD_DIM), 0)
        for slot in slots:
            for j in range(groups):
                live = place < linked_rows(ranks[slot], j)
                key = branch[slot, j, 0, :, cols].astype(jnp.float32)
                value = branch[slot, j, 1, :, cols].astype(jnp.float32)
                keys.append(jnp.where(live, key, first_key).astype(jnp.bfloat16))
                values.append(
                    jnp.concatenate([jnp.where(live, value, 0.0), jnp.where(live, 1.0, 0.0)], 1).astype(jnp.bfloat16)
                )
        return jnp.concatenate(keys, 0), jnp.concatenate(values, 0)

    def prompt_operands(pieces, h):
        cols = slice(h * HEAD_DIM, (h + 1) * HEAD_DIM)
        blocks = [own_prompt.at[:] if j == 0 else prompt.at[:, j - 1] for j in pieces]
        keys, values = [jnp.concatenate([block[kind, :, cols] for block in blocks], 0) for kind in range(2)]
        return keys, jnp.concatenate([values, jnp.ones_like(values)], 1)

    def joined(*pairs):
        return [jnp.concatenate(side, 0) for side in zip(*pairs)]

    def attend(h, keys, values, first=False, last=False):
        count = keys.shape[0]
        heads = block_rows // rows
        for start in range(0, sub, heads):
            span = slice(start * rows, (start + heads) * rows)
            query = jnp.concatenate(
                [q_ref[:, (h * sub + i) * HEAD_DIM:(h * sub + i + 1) * HEAD_DIM] for i in range(start, start + heads)], 0
            )
            scores = lax.dot_general(query, keys, (((1,), (1,)), ((), ())), preferred_element_type=jnp.float32)
            tiles = [scores[:, t:min(t + HEAD_DIM, count)] for t in range(0, count, HEAD_DIM)]
            if first:
                causal = lax.broadcasted_iota(jnp.int32, (block_rows, HEAD_DIM), 1) <= (
                    lax.broadcasted_iota(jnp.int32, (block_rows, HEAD_DIM), 0) % rows
                )
                tiles[0] = jnp.where(causal, tiles[0], HIDDEN)
            full = [tile for tile in tiles if tile.shape[1] == HEAD_DIM]
            peak = jnp.max(functools.reduce(jnp.maximum, full), -1, keepdims=True)
            for tile in tiles[len(full):]:
                peak = jnp.maximum(peak, jnp.max(tile, -1, keepdims=True))
            if first:
                peak = jnp.broadcast_to(peak, (block_rows, HEAD_DIM))
            else:
                former = peak_ref[h, span]
                peak = jnp.maximum(former, peak)
            weights = jnp.concatenate([jnp.exp2((tile - peak[:, :tile.shape[1]]) * EXP2_SCALE).astype(jnp.bfloat16) for tile in tiles], 1)
            both = lax.dot_general(weights, values, (((1,), (0,)), ((), ())), preferred_element_type=jnp.float32)
            acc, tot = both[:, :HEAD_DIM], both[:, HEAD_DIM:]
            if not first:
                scale = jnp.exp2((former - peak) * EXP2_SCALE)
                acc = acc + acc_ref[h, span] * scale
                tot = tot + tot_ref[h, span] * scale
            if last:
                result = (acc / tot).astype(jnp.bfloat16)
                for i in range(heads):
                    head = h * sub + start + i
                    out_ref[:, head * HEAD_DIM:(head + 1) * HEAD_DIM] = result[i * rows:(i + 1) * rows]
            else:
                peak_ref[h, span] = peak
                acc_ref[h, span] = acc
                tot_ref[h, span] = tot

    loads[0].wait()
    if groups == 1:
        loads[1].wait()
    for load in loads[2:]:
        load.wait()
    for kind in range(2):
        branch_arrived(SIB, kind)
    for h in range(kv_per):
        attend(h, *joined(operands([OWN, SIB], h), prompt_operands([0], h)), first=True)
    pass_branch(A, SIB_A)
    pass_branch(B, SIB_B)
    for slot in (SIB_A, SIB_B):
        for kind in range(2):
            branch_arrived(slot, kind)
    for h in range(kv_per):
        attend(h, *operands([A, B, SIB_A, SIB_B], h))
        if h == 0:
            pass_branch(DIAG, SIB_DIAG)
    for kind in range(2):
        branch_arrived(SIB_DIAG, kind)
    for h in range(kv_per):
        attend(h, *operands([DIAG, SIB_DIAG], h))
    for j in reversed(order):
        pass_prompt(j)
    for j in order:
        prompt_passed(j)
    for h in range(kv_per):
        attend(h, *prompt_operands(order, h), last=True)
    for copy in sent:
        copy.wait_send()


def local(queries, branch_kv, prompt_kv, ancestry, segment_of_slot, counts):
    seg_count = lax.axis_size("seg")
    stretch_count = lax.axis_size("stretch")
    rows, features = queries.shape
    per_dev = features // HEAD_DIM
    kv_per = max(1, per_dev // GROUP)
    sub = per_dev // kv_per
    width = kv_per * HEAD_DIM
    groups = seg_count // CUBE
    state = pltpu.VMEM((kv_per, sub * rows, HEAD_DIM), jnp.float32)
    dma = pltpu.SemaphoreType.DMA
    hbm = pl.BlockSpec(memory_space=pl.ANY)
    return pl.pallas_call(
        functools.partial(kernel, seg_count, stretch_count, min(sub, 8) * rows),
        out_shape=jax.ShapeDtypeStruct((rows, features), jnp.bfloat16),
        in_specs=[hbm] * 6,
        out_specs=pl.BlockSpec(memory_space=pltpu.VMEM),
        scratch_shapes=[
            pltpu.SMEM(ancestry.shape, jnp.int32),
            pltpu.SMEM(segment_of_slot.shape, jnp.int32),
            pltpu.SMEM(counts.shape, jnp.int32),
            pltpu.VMEM((rows, features), jnp.bfloat16),
            pltpu.VMEM((2, prompt_kv.shape[1], width), jnp.bfloat16),
            pltpu.VMEM((CUBE, groups, 2, rows, width), jnp.bfloat16),
            pltpu.VMEM((2, stretch_count - 1, prompt_kv.shape[1], width), jnp.bfloat16),
            state, state, state,
            dma((6,)),
            dma((stretch_count - 1,)), dma((stretch_count - 1,)),
            dma((max(1, groups - 1),)), dma((max(1, groups - 1),)),
            dma((8, 2)), dma((8, 2)),
            dma((stretch_count - 1,)), dma((stretch_count - 1,)),
        ],
        compiler_params=pltpu.CompilerParams(
            collective_id=0, has_side_effects=True, vmem_limit_bytes=62 * 1024 * 1024
        ),
    )(ancestry, segment_of_slot, counts, queries, branch_kv, prompt_kv)


def solution(mesh):
    return jax.shard_map(
        local,
        mesh=mesh,
        in_specs=(
            P("seg", "stretch"),
            P(None, "seg", None),
            P(None, "stretch", None),
            P(),
            P(),
            P(),
        ),
        out_specs=P("seg", "stretch"),
        check_vma=False,
    )
```

```python
import functools
import math

import jax
import jax.numpy as jnp
from jax import lax
from jax.experimental import pallas as pl
from jax.experimental.pallas import tpu as pltpu
from jax.sharding import PartitionSpec as P

HEADS = 64
KV_HEADS = 8
HEAD_DIM = 128
GROUP = HEADS // KV_HEADS
CUBE = 8
EXP2_SCALE = math.log2(math.e) / math.sqrt(HEAD_DIM)
HIDDEN = -1e30

OWN, SIB, A, B, SIB_A, SIB_B, DIAG, SIB_DIAG = range(8)


def kernel(
    seg_count, stretch_count, block_rows,
    anc_hbm, seg_hbm, cnt_hbm, q_hbm, branch_hbm, prompt_hbm, out_ref,
    anc_ref, seg_ref, cnt_ref,
    q_ref, own_prompt, branch, prompt, peak_ref, acc_ref, tot_ref,
    local_sem, z_send, z_recv, g_send, g_recv, b_send, b_recv, p_send, p_recv,
):
    per_dev = q_hbm.shape[1] // HEAD_DIM
    rows = q_hbm.shape[0]
    kv_per = max(1, per_dev // GROUP)
    sub = per_dev // kv_per
    width = kv_per * HEAD_DIM
    groups = seg_count // CUBE

    s = lax.axis_index("seg")
    z = lax.axis_index("stretch")
    g, r = s // CUBE, s % CUBE
    c = r % 2
    y, x = r // 4, (r // 2) % 2
    dx, dy, dc = 2 - 4 * x, 4 - 8 * y, 1 - 2 * c
    da = (1 - c) * dx + c * dy
    db = c * dx + (1 - c) * dy
    to_a, to_b, to_sib = {"seg": s + da}, {"seg": s + db}, {"seg": s + dc}
    to_diag = {"seg": s + da + db}

    def columns(stretch):
        first = stretch * per_dev // GROUP
        return pl.ds(pl.multiple_of(first * HEAD_DIM, HEAD_DIM), width)

    loads = [
        pltpu.make_async_copy(q_hbm, q_ref, local_sem.at[0]),
        pltpu.make_async_copy(branch_hbm.at[:, :, columns(z)], branch.at[OWN, 0], local_sem.at[1]),
        pltpu.make_async_copy(prompt_hbm.at[:, :, columns(z)], own_prompt, local_sem.at[2]),
        pltpu.make_async_copy(anc_hbm, anc_ref, local_sem.at[3]),
        pltpu.make_async_copy(seg_hbm, seg_ref, local_sem.at[4]),
        pltpu.make_async_copy(cnt_hbm, cnt_ref, local_sem.at[5]),
    ]
    barrier = pltpu.get_barrier_semaphore()
    partners = [to_a, to_b, to_sib, to_diag]
    partners += [{"stretch": (z + j) % stretch_count} for j in range(1, stretch_count)]
    partners += [{"seg": (g + j) % groups * CUBE + r} for j in range(1, groups)]
    for partner in partners:
        pl.semaphore_signal(barrier, inc=1, device_id=partner, device_id_type=pl.DeviceIdType.MESH)
    for load in loads:
        load.start()
    pl.semaphore_wait(barrier, len(partners))

    sent = []

    def send(source, target, send_sem, recv_sem, device):
        copy = pltpu.make_async_remote_copy(
            src_ref=source, dst_ref=target, send_sem=send_sem, recv_sem=recv_sem,
            device_id=device, device_id_type=pl.DeviceIdType.MESH,
        )
        copy.start()
        sent.append(copy)

    def arrived(target, recv_sem):
        pltpu.make_async_copy(target, target, recv_sem).wait()

    order = list(range(1, stretch_count))
    order.sort(key=lambda j: -abs(2 * j - stretch_count))
    for j in order:
        other = (z + stretch_count - j) % stretch_count
        send(
            prompt_hbm.at[c, :, columns(other)], prompt.at[c, j - 1],
            z_send.at[j - 1], z_recv.at[j - 1], {"stretch": other},
        )
    for j in range(1, groups):
        send(
            branch_hbm.at[:, :, columns(z)], branch.at[OWN, j],
            g_send.at[j - 1], g_recv.at[j - 1], {"seg": (g + groups - j) % groups * CUBE + r},
        )
    if groups > 1:
        loads[1].wait()
        for j in range(1, groups):
            arrived(branch.at[OWN, j], g_recv.at[j - 1])

    def branch_part(slot, kind):
        return branch.at[slot, :, kind]

    def send_branch(slot, kind, target, device):
        if groups == 1 and slot == OWN:
            source = branch_hbm.at[kind, :, columns(z)]
            place = branch.at[target, 0, kind]
        else:
            source, place = branch_part(slot, kind), branch_part(target, kind)
        send(source, place, b_send.at[target, kind], b_recv.at[target, kind], device)

    def branch_arrived(slot, kind):
        arrived(branch_part(slot, kind), b_recv.at[slot, kind])

    for kind in range(2):
        send_branch(OWN, kind, A, to_a)
        send_branch(OWN, kind, SIB, to_sib)
    for kind in range(2):
        send_branch(OWN, kind, B, to_b)
    for kind in range(2):
        send_branch(OWN, kind, DIAG, to_diag)

    def pass_prompt(j):
        arrived(prompt.at[c, j - 1], z_recv.at[j - 1])
        send(prompt.at[c, j - 1], prompt.at[c, j - 1], p_send.at[j - 1], p_recv.at[j - 1], to_sib)

    def pass_branch(slot, target):
        for kind in range(2):
            branch_arrived(slot, kind)
            send_branch(slot, kind, target, to_sib)

    def prompt_passed(j):
        arrived(prompt.at[1 - c, j - 1], p_recv.at[j - 1])

    def linked_rows(rank, j):
        slot = (g + j) % groups * CUBE + rank
        segment = seg_ref[slot]
        return anc_ref[seg_ref[s], segment] * cnt_ref[segment]

    ranks = {
        OWN: r, SIB: r + dc, A: r + da, B: r + db, SIB_A: r + dc + db, SIB_B: r + dc + da,
        DIAG: r + da + db, SIB_DIAG: r + dc + da + db,
    }
    ones = jnp.ones((1, HEAD_DIM), jnp.float32)

    def operands(slots, h):
        cols = slice(h * HEAD_DIM, (h + 1) * HEAD_DIM)
        first_key = own_prompt[0, 0:16, cols].astype(jnp.float32)[0:1]
        keys, values = [], []
        place = lax.broadcasted_iota(jnp.int32, (rows, HEAD_DIM), 0)
        for slot in slots:
            for j in range(groups):
                live = place < linked_rows(ranks[slot], j)
                key = branch[slot, j, 0, :, cols].astype(jnp.float32)
                value = branch[slot, j, 1, :, cols].astype(jnp.float32)
                keys.append(jnp.where(live, key, first_key).astype(jnp.bfloat16))
                values.append(
                    jnp.concatenate([jnp.where(live, value, 0.0), jnp.where(live, 1.0, 0.0)], 1).astype(jnp.bfloat16)
                )
        return jnp.concatenate(keys, 0), jnp.concatenate(values, 0)

    def prompt_operands(pieces, h):
        cols = slice(h * HEAD_DIM, (h + 1) * HEAD_DIM)
        blocks = [own_prompt.at[:] if j == 0 else prompt.at[:, j - 1] for j in pieces]
        keys, values = [jnp.concatenate([block[kind, :, cols] for block in blocks], 0) for kind in range(2)]
        return keys, jnp.concatenate([values, jnp.ones_like(values)], 1)

    def joined(*pairs):
        return [jnp.concatenate(side, 0) for side in zip(*pairs)]

    def attend(h, keys, values, first=False, last=False):
        count = keys.shape[0]
        heads = block_rows // rows
        for start in range(0, sub, heads):
            span = slice(start * rows, (start + heads) * rows)
            query = jnp.concatenate(
                [q_ref[:, (h * sub + i) * HEAD_DIM:(h * sub + i + 1) * HEAD_DIM] for i in range(start, start + heads)], 0
            )
            scores = lax.dot_general(query, keys, (((1,), (1,)), ((), ())), preferred_element_type=jnp.float32)
            tiles = [scores[:, t:min(t + HEAD_DIM, count)] for t in range(0, count, HEAD_DIM)]
            if first:
                causal = lax.broadcasted_iota(jnp.int32, (block_rows, HEAD_DIM), 1) <= (
                    lax.broadcasted_iota(jnp.int32, (block_rows, HEAD_DIM), 0) % rows
                )
                tiles[0] = jnp.where(causal, tiles[0], HIDDEN)
            full = [tile for tile in tiles if tile.shape[1] == HEAD_DIM]
            peak = jnp.max(functools.reduce(jnp.maximum, full), -1, keepdims=True)
            for tile in tiles[len(full):]:
                peak = jnp.maximum(peak, jnp.max(tile, -1, keepdims=True))
            if first:
                peak = jnp.broadcast_to(peak, (block_rows, HEAD_DIM))
            else:
                former = peak_ref[h, span]
                peak = jnp.maximum(former, peak)
            weights = jnp.concatenate([jnp.exp2((tile - peak[:, :tile.shape[1]]) * EXP2_SCALE).astype(jnp.bfloat16) for tile in tiles], 1)
            both = lax.dot_general(weights, values, (((1,), (0,)), ((), ())), preferred_element_type=jnp.float32)
            acc, tot = both[:, :HEAD_DIM], both[:, HEAD_DIM:]
            if not first:
                scale = jnp.exp2((former - peak) * EXP2_SCALE)
                acc = acc + acc_ref[h, span] * scale
                tot = tot + tot_ref[h, span] * scale
            if last:
                result = (acc / tot).astype(jnp.bfloat16)
                for i in range(heads):
                    head = h * sub + start + i
                    out_ref[:, head * HEAD_DIM:(head + 1) * HEAD_DIM] = result[i * rows:(i + 1) * rows]
            else:
                peak_ref[h, span] = peak
                acc_ref[h, span] = acc
                tot_ref[h, span] = tot

    loads[0].wait()
    if groups == 1:
        loads[1].wait()
    for load in loads[2:]:
        load.wait()
    for kind in range(2):
        branch_arrived(SIB, kind)
    for h in range(kv_per):
        attend(h, *joined(operands([OWN, SIB], h), prompt_operands([0], h)), first=True)
    pass_branch(A, SIB_A)
    pass_branch(B, SIB_B)
    for slot in (SIB_A, SIB_B):
        for kind in range(2):
            branch_arrived(slot, kind)
    for h in range(kv_per):
        attend(h, *operands([A, B, SIB_A, SIB_B], h))
        if h == 0:
            pass_branch(DIAG, SIB_DIAG)
    for kind in range(2):
        branch_arrived(SIB_DIAG, kind)
    for h in range(kv_per):
        attend(h, *operands([DIAG, SIB_DIAG], h))
    for j in order:
        pass_prompt(j)
    for j in order:
        prompt_passed(j)
    for h in range(kv_per):
        attend(h, *prompt_operands(order, h), last=True)
    for copy in sent:
        copy.wait_send()


def local(queries, branch_kv, prompt_kv, ancestry, segment_of_slot, counts):
    seg_count = lax.axis_size("seg")
    stretch_count = lax.axis_size("stretch")
    rows, features = queries.shape
    per_dev = features // HEAD_DIM
    kv_per = max(1, per_dev // GROUP)
    sub = per_dev // kv_per
    width = kv_per * HEAD_DIM
    groups = seg_count // CUBE
    state = pltpu.VMEM((kv_per, sub * rows, HEAD_DIM), jnp.float32)
    dma = pltpu.SemaphoreType.DMA
    hbm = pl.BlockSpec(memory_space=pl.ANY)
    return pl.pallas_call(
        functools.partial(kernel, seg_count, stretch_count, min(sub, 8) * rows),
        out_shape=jax.ShapeDtypeStruct((rows, features), jnp.bfloat16),
        in_specs=[hbm] * 6,
        out_specs=pl.BlockSpec(memory_space=pltpu.VMEM),
        scratch_shapes=[
            pltpu.SMEM(ancestry.shape, jnp.int32),
            pltpu.SMEM(segment_of_slot.shape, jnp.int32),
            pltpu.SMEM(counts.shape, jnp.int32),
            pltpu.VMEM((rows, features), jnp.bfloat16),
            pltpu.VMEM((2, prompt_kv.shape[1], width), jnp.bfloat16),
            pltpu.VMEM((CUBE, groups, 2, rows, width), jnp.bfloat16),
            pltpu.VMEM((2, stretch_count - 1, prompt_kv.shape[1], width), jnp.bfloat16),
            state, state, state,
            dma((6,)),
            dma((stretch_count - 1,)), dma((stretch_count - 1,)),
            dma((max(1, groups - 1),)), dma((max(1, groups - 1),)),
            dma((8, 2)), dma((8, 2)),
            dma((stretch_count - 1,)), dma((stretch_count - 1,)),
        ],
        compiler_params=pltpu.CompilerParams(
            collective_id=0, has_side_effects=True, vmem_limit_bytes=62 * 1024 * 1024
        ),
    )(ancestry, segment_of_slot, counts, queries, branch_kv, prompt_kv)


def solution(mesh):
    return jax.shard_map(
        local,
        mesh=mesh,
        in_specs=(
            P("seg", "stretch"),
            P(None, "seg", None),
            P(None, "stretch", None),
            P(),
            P(),
            P(),
        ),
        out_specs=P("seg", "stretch"),
        check_vma=False,
    )
```
